1024 devices in a mesh: dp: 64 (over y, z), mp: 16 (over x, core).
Axes of the slice: x: 8, y: 8, z: 8, core: 2. Of those that a mesh axis runs over, the one named last changes fastest.
Arguments:
- cotangent: bfloat16 [16384, 5376], P('dp', 'mp')
- token_ids: int32 [16384], P('dp'), may hold values from 0 to 32767, as said below
- block_counts: int32 [64, 128], P('dp'), may hold values from 0 to 8, as said below
- block_slot: int32 [128], replicated, may hold values from 0 to 127, as said below
- table: bfloat16 [32768, 5376], P('dp', 'mp'), may hold values from -6 to 6
- m_code: bfloat16 [32768, 5376], P('dp', 'mp'), may hold values from -1 to 1
- m_scale: float32 [32768], P('dp'), may hold values from 0.05 to 0.5
- v_code: bfloat16 [32768, 5376], P('dp', 'mp'), may hold values from 0.25 to 1
- v_scale: float32 [32768], P('dp'), may hold values from 0.3 to 3
Outputs:
- new_table: bfloat16 [32768, 5376], P('dp', 'mp')
- new_m_code: bfloat16 [32768, 5376], P('dp', 'mp')
- new_m_scale: float32 [32768], P('dp')
- new_v_code: bfloat16 [32768, 5376], P('dp', 'mp')
- new_v_scale: float32 [32768], P('dp')
The draws below stay inside these ranges and needn't reach their ends.
Inputs may be any that keep to these rules, and one draw needn't show every extreme that they name: `token_ids`: within each shard of 256 tokens the ids are sorted ascending. block_counts[d, b] is the number of ids of shard d in vocabulary block b (ids b * 256 to b * 256 + 255), so each row sums to 256. The table rows of vocabulary block b lie on index block_slot[b] // 2 of dp; the tokens of one shard whose rows lie on one index of dp number at most 8. `block_slot`: A permutation of 0 to 127.
All inputs are finite; a program needn't handle non-finite values. Where the reference program divides by a largest or mean magnitude, that divisor is 1e-20 or more.
Results may differ from the reference program's by a relative error of at most 0.0025.
Values may be sent and summed in bfloat16 or wider, within the bound.
A program may use at most 32 MiB of HBM per device.

```python
import math
import jax
import jax.numpy as jnp
from jax import lax

D = 5376
BLOCK = 256
TOK_DEV = 256
ROWS_OWN = 512
NB = 128
V = 32768
TOKENS = 16384
N_DP = 64


def routing_tables(key):
    key_hot, key_slot, key_shards = jax.random.split(key, 3)
    slot_perm = jax.random.permutation(key_slot, NB).astype(jnp.int32)
    vocab_of = jnp.zeros((NB,), jnp.int32).at[slot_perm].set(jnp.arange(NB, dtype=jnp.int32))
    hot_owner = jax.random.randint(key_hot, (), 0, N_DP)
    mean_load = TOK_DEV // N_DP

    def shard_draw(shard_key):
        key_order, key_lift, key_reach, key_rows = jax.random.split(shard_key, 4)
        order = jax.random.permutation(key_order, N_DP).astype(jnp.int32)
        rank_of = jnp.zeros((N_DP,), jnp.int32).at[order].set(jnp.arange(N_DP, dtype=jnp.int32))
        follow = order[(rank_of + 1) % N_DP]
        lift = jax.random.randint(key_lift, (N_DP,), 0, mean_load + 1)
        lift = lift.at[hot_owner].set(mean_load)
        lift = lift.at[follow[hot_owner]].set(0)
        owner_load = mean_load + lift - lift[follow]
        load_ends = jnp.cumsum(owner_load)
        position = jnp.arange(TOK_DEV, dtype=jnp.int32)
        owner_of = jnp.sum((position[:, None] >= load_ends[None, :]).astype(jnp.int32), axis=1)
        reach = jax.random.randint(key_reach, (TOK_DEV,), 1, ROWS_OWN + 1)
        reach = jnp.where(owner_of == hot_owner, jnp.minimum(reach, BLOCK), reach)
        local_row = jax.random.randint(key_rows, (TOK_DEV,), 0, reach)
        stored_row = owner_of * ROWS_OWN + local_row
        shard_ids = vocab_of[stored_row // BLOCK] * BLOCK + stored_row % BLOCK
        shard_ids = jnp.sort(shard_ids).astype(jnp.int32)
        shard_counts = jnp.sum((shard_ids[:, None] // BLOCK == jnp.arange(NB, dtype=jnp.int32)[None, :]).astype(jnp.int32), axis=0)
        return (shard_ids, shard_counts.astype(jnp.int32))
    all_ids, all_counts = jax.vmap(shard_draw)(jax.random.split(key_shards, N_DP))
    return (all_ids.reshape(-1), all_counts, slot_perm)


def draw_token_ids(key, part):
    return routing_tables(key)[0]


def draw_block_counts(key, part):
    return routing_tables(key)[1]


def draw_block_slot(key, part):
    return routing_tables(key)[2]


def draw_cotangent(key, part):
    key = jax.random.fold_in(key, 11)
    key_base, key_cols, key_tok = jax.random.split(key, 3)
    col_ramp = jnp.exp(math.log(3.0) * jnp.arange(D, dtype=jnp.float32) / D)
    col_scale = jnp.exp(jax.random.uniform(key_cols, (D,), jnp.float32, 0.0, math.log(10.0))) * col_ramp
    tok_scale = jnp.exp(jax.random.uniform(key_tok, (TOKENS, 1), jnp.float32, 0.0, math.log(4.0)))
    base = jax.random.normal(key_base, (TOKENS, D), jnp.float32)
    factor = 0.1
    return (factor * base * col_scale[None, :] * tok_scale).astype(jnp.bfloat16)


def block_scale(key, dims, shards, smallest, largest):
    loudness, own = 1.0, jax.random.fold_in(key, 6)
    for dim, parts in shards:
        steps = jnp.exp(jax.random.uniform(jax.random.fold_in(own, dim), (parts,), jnp.float32, smallest / len(shards), largest / len(shards)))
        loudness = loudness * jnp.repeat(steps, dims[dim] // parts).reshape([-1 if axis == dim else 1 for axis in range(len(dims))])
    return loudness


def noise(key, shape, scale, most, shards=(), kind=jnp.bfloat16):
    result = jax.random.normal(key, shape, jnp.float32) * scale
    if len(shards) > 0:
        result = block_scale(key, shape, shards, -0.22, 0.18) * result
    return jnp.clip(result, min=-most, max=most).astype(kind)


def setup_inputs(seed: int = 0) -> dict:
    streams_of = jax.random.split(jax.random.key(seed), 10)
    cotangent = draw_cotangent(jax.random.fold_in(streams_of[9], 71), 0)
    token_ids = draw_token_ids(jax.random.fold_in(streams_of[9], 71), 0)
    block_counts = draw_block_counts(jax.random.fold_in(streams_of[9], 71), 0)
    block_slot = draw_block_slot(jax.random.fold_in(streams_of[9], 71), 0)
    table = noise(streams_of[4], (V, D), 1.0, 6.0, ((0, 64), (1, 16)))
    m_code = jnp.clip(jax.random.uniform(streams_of[5], (V, D), jnp.float32, -1.0, 1.0) * block_scale(streams_of[5], (V, D), ((0, 64), (1, 16)), -0.4, 0.0), -1.0, 1.0).astype(jnp.bfloat16)
    m_scale = jnp.clip(jnp.exp(math.log(0.5) - 2.3025851 * jax.random.uniform(streams_of[6], (V,), jnp.float32) ** block_scale(streams_of[6], (V,), ((0, 64),), -0.2, 0.2)), 0.05, 0.5)
    v_code = jnp.clip(0.25 + 0.75 * jax.random.uniform(streams_of[7], (V, D), jnp.float32) ** block_scale(streams_of[7], (V, D), ((0, 64), (1, 16)), -0.2, 0.2), 0.25, 1.0).astype(jnp.bfloat16)
    v_scale = jnp.clip(jnp.exp(math.log(3.0) - 2.3025851 * jax.random.uniform(streams_of[8], (V,), jnp.float32) ** block_scale(streams_of[8], (V,), ((0, 64),), -0.2, 0.2)), 0.3, 3.0)
    return dict(cotangent=cotangent, token_ids=token_ids, block_counts=block_counts, block_slot=block_slot, table=table, m_code=m_code, m_scale=m_scale, v_code=v_code, v_scale=v_scale)


beta_first = 0.9
beta_second = 0.95
step_rate = 0.05
eps_root = 1e-08
eps_peak = 1e-06

def moments(gradient, table_cols, mcode_cols, mscale, vcode_cols, vscale):
    moment = beta_first * (mcode_cols.astype(jnp.float32) * mscale[:, None]) + 0.1 * gradient
    second = beta_second * (vcode_cols.astype(jnp.float32) * vscale[:, None]) + 0.05 * (gradient * gradient)
    updated = (table_cols.astype(jnp.float32) - step_rate * (moment / (jnp.sqrt(second) + eps_root))).astype(jnp.bfloat16)
    return (updated, moment, second)

def reference(cotangent, token_ids, block_counts, block_slot, table, m_code, m_scale, v_code, v_scale):
    block_ends = jnp.cumsum(block_counts, axis=1).astype(jnp.int32)
    position = jnp.arange(TOK_DEV, dtype=jnp.int32)
    blocks = lax.optimization_barrier(jnp.sum((position[None, :, None] >= block_ends[:, None, :]).astype(jnp.int32), axis=2)).astype(jnp.int32)
    blocks = jnp.minimum(blocks, NB - 1).reshape(-1)
    table_rows = (jnp.take(block_slot, blocks) * BLOCK + token_ids % BLOCK).astype(jnp.int32)
    col_width = D // 16

    def column_block(group_index):
        first_col = group_index * col_width

        def columns_of(array):
            return lax.dynamic_slice_in_dim(array, first_col, col_width, 1)
        gradient = jax.ops.segment_sum(columns_of(cotangent).astype(jnp.float32), table_rows, num_segments=V)
        return moments(gradient, columns_of(table), columns_of(m_code), m_scale, columns_of(v_code), v_scale)
    updated, moment, second = lax.map(column_block, jnp.arange(16, dtype=jnp.int32))

    def joined(stacked):
        return jnp.moveaxis(stacked, 0, 1).reshape(V, D)
    new_table = joined(updated)
    moment = joined(moment)
    second = joined(second)
    new_m_scale = lax.optimization_barrier(jnp.max(jnp.abs(moment), axis=1))
    new_v_scale = lax.optimization_barrier(jnp.max(second, axis=1))
    new_m_code = (moment / (new_m_scale[:, None] + eps_peak)).astype(jnp.bfloat16)
    new_v_code = (second / (new_v_scale[:, None] + eps_peak)).astype(jnp.bfloat16)
    return (new_table, new_m_code, new_m_scale, new_v_code, new_v_scale)
```

```python
import functools

import jax
import jax.numpy as jnp
from jax import lax
from jax.experimental import pallas as pl
from jax.experimental.pallas import tpu as pltpu
from jax.sharding import PartitionSpec as P

BLOCK = 256
CAP = 8
LANES = 128
MESH = pl.DeviceIdType.MESH

beta_first = 0.9
beta_second = 0.95
step_rate = 0.05
eps_root = 1e-08
eps_peak = 1e-06


def kernel(
    n_dp, n_mp,
    cot_hbm, tok_hbm, slot_hbm, tab_hbm, mc_hbm, ms_hbm, vc_hbm, vs_hbm,
    nt_hbm, nm_hbm, nms_hbm, nv_hbm, nvs_hbm,
    cot, tok, slot, tab, mc, ms, vc, vs,
    send, recv, mom, sec, peak, peaks, nt, nm, nv, nms, nvs,
    in_sems, out_sems, send_sem, recv_sem, psend_sem, precv_sem,
):
    dp, mp = lax.axis_index("dp"), lax.axis_index("mp")
    width, n_tok = cot.shape
    rows = tab.shape[1]
    n_blk = slot.shape[1]
    n_slot = n_dp * CAP
    full = send.shape[2]
    n_meta = full - width
    strip = 48 if width % 48 == 0 else 16

    barrier = pltpu.get_barrier_semaphore()

    def greet_dp(i, _):
        pl.semaphore_signal(barrier, inc=1, device_id={"dp": lax.rem(dp + i, n_dp)}, device_id_type=MESH)
        return 0

    def greet_mp(i, _):
        pl.semaphore_signal(barrier, inc=1, device_id={"mp": lax.rem(mp + i, n_mp)}, device_id_type=MESH)
        return 0

    copies = [
        pltpu.make_async_copy(src, dst, in_sems.at[i])
        for i, (src, dst) in enumerate(
            ((tok_hbm, tok), (slot_hbm, slot), (cot_hbm, cot), (ms_hbm, ms), (vs_hbm, vs), (mc_hbm, mc), (vc_hbm, vc), (tab_hbm, tab))
        )
    ]
    for copy in copies:
        copy.start()
    lax.fori_loop(1, n_dp, greet_dp, 0)
    lax.fori_loop(1, n_mp, greet_mp, 0)

    copies[0].wait()
    copies[1].wait()
    ids = tok[...]
    low = ids % BLOCK
    blk = ids // BLOCK
    in_block = (lax.broadcasted_iota(jnp.int32, (n_blk, n_tok), 0) == blk).astype(jnp.bfloat16)
    slot_rows = jnp.broadcast_to(slot[...].astype(jnp.float32), (16, n_blk)).astype(jnp.bfloat16)
    held = jnp.dot(slot_rows, in_block, preferred_element_type=jnp.float32)[0:1, :].astype(jnp.int32)
    owner = held // 2
    sub = held % 2
    of_owner = (lax.broadcasted_iota(jnp.int32, (n_dp, n_tok), 0) == owner).astype(jnp.float32)
    earlier = (
        lax.broadcasted_iota(jnp.int32, (n_tok, n_tok), 0) < lax.broadcasted_iota(jnp.int32, (n_tok, n_tok), 1)
    ).astype(jnp.bfloat16)
    before = jnp.dot(of_owner.astype(jnp.bfloat16), earlier, preferred_element_type=jnp.float32)
    rank = jnp.sum(of_owner * before, axis=0, keepdims=True)
    place = owner * CAP + rank.astype(jnp.int32)
    chosen = (lax.broadcasted_iota(jnp.int32, (n_slot, n_tok), 0) == place).astype(jnp.bfloat16)

    meta_row = lax.broadcasted_iota(jnp.int32, (n_meta, n_tok), 0)
    meta = jnp.where(meta_row == 0, low, jnp.where(meta_row == 1, (sub + 1) * BLOCK, 0))
    meta = meta.astype(jnp.float32).astype(jnp.bfloat16)
    copies[2].wait()
    tokens = jnp.concatenate([cot[...], meta], axis=0)
    sent = lax.dot_general(chosen, tokens, (((1,), (1,)), ((), ())), preferred_element_type=jnp.float32)
    send[...] = sent.reshape(n_dp, CAP, full).astype(jnp.bfloat16)

    pl.semaphore_wait(barrier, n_dp + n_mp - 2)

    def send_rows(i, _):
        to = lax.rem(dp + i, n_dp)
        pltpu.make_async_remote_copy(
            src_ref=send.at[to], dst_ref=recv.at[dp], send_sem=send_sem, recv_sem=recv_sem,
            device_id={"dp": to}, device_id_type=MESH,
        ).start()
        return 0

    lax.fori_loop(1, n_dp, send_rows, 0)
    recv[pl.ds(dp, 1)] = send[pl.ds(dp, 1)]

    for copy in copies[3:]:
        copy.wait()
    for c in range(0, width, strip):
        at = pl.ds(c, strip)
        mom[at, :] = beta_first * (mc[at, :].astype(jnp.float32) * ms[...])
        sec[at, :] = beta_second * (vc[at, :].astype(jnp.float32) * vs[...])

    others = pl.ds(0, n_dp - 1)
    pltpu.make_async_copy(recv.at[others], recv.at[others], recv_sem).wait()

    got = recv[...].astype(jnp.float32).reshape(n_slot, full).astype(jnp.bfloat16)
    last = full - LANES
    pick = (lax.broadcasted_iota(jnp.int32, (LANES, rows), 0) >= width - last).astype(jnp.bfloat16)
    index = jnp.dot(got[:, last:full], pick, preferred_element_type=jnp.float32).astype(jnp.int32)
    row = lax.broadcasted_iota(jnp.int32, (n_slot, rows), 1) + BLOCK
    selector = (row == index).astype(jnp.bfloat16)
    grad = lax.dot_general(got, selector, (((0,), (0,)), ((), ())), preferred_element_type=jnp.float32)

    m_top = jnp.zeros((8, rows), jnp.float32)
    v_top = jnp.zeros((8, rows), jnp.float32)
    for c in range(0, width, strip):
        at = pl.ds(c, strip)
        g = grad[c : c + strip]
        moment = mom[at, :] + 0.1 * g
        second = sec[at, :] + 0.05 * (g * g)
        mom[at, :] = moment
        sec[at, :] = second
        m_top = jnp.maximum(m_top, jnp.max(jnp.abs(moment).reshape(strip // 8, 8, rows), axis=0))
        v_top = jnp.maximum(v_top, jnp.max(second.reshape(strip // 8, 8, rows), axis=0))
    peak[0:1, :] = jnp.max(m_top, axis=0, keepdims=True)
    peak[1:2, :] = jnp.max(v_top, axis=0, keepdims=True)

    def send_peak(i, _):
        to = lax.rem(mp + i, n_mp)
        pltpu.make_async_remote_copy(
            src_ref=peak, dst_ref=peaks.at[mp], send_sem=psend_sem, recv_sem=precv_sem,
            device_id={"mp": to}, device_id_type=MESH,
        ).start()
        return 0

    lax.fori_loop(1, n_mp, send_peak, 0)
    peaks[pl.ds(mp, 1)] = peak[...][None]

    for c in range(0, width, strip):
        at = pl.ds(c, strip)
        moment, second = mom[at, :], sec[at, :]
        nt[at, :] = (tab[at, :].astype(jnp.float32) - step_rate * (moment / (jnp.sqrt(second) + eps_root))).astype(jnp.bfloat16)
    outs = [
        pltpu.make_async_copy(src, dst, out_sems.at[i])
        for i, (src, dst) in enumerate(((nt, nt_hbm), (nms, nms_hbm), (nvs, nvs_hbm), (nm, nm_hbm), (nv, nv_hbm)))
    ]
    outs[0].start()

    others = pl.ds(0, n_mp - 1)
    pltpu.make_async_copy(peaks.at[others], peaks.at[others], precv_sem).wait()
    top = jnp.max(peaks[...], axis=0)
    m_peak, v_peak = top[0:1], top[1:2]
    nms[...] = m_peak
    nvs[...] = v_peak
    outs[1].start()
    outs[2].start()
    m_peak, v_peak = m_peak + eps_peak, v_peak + eps_peak
    for c in range(0, width, strip):
        at = pl.ds(c, strip)
        nm[at, :] = (mom[at, :] / m_peak).astype(jnp.bfloat16)
        nv[at, :] = (sec[at, :] / v_peak).astype(jnp.bfloat16)
    outs[3].start()
    outs[4].start()
    pltpu.make_async_copy(peaks.at[others], peaks.at[others], psend_sem).wait()
    others = pl.ds(0, n_dp - 1)
    pltpu.make_async_copy(send.at[others], send.at[others], send_sem).wait()
    for out in outs:
        out.wait()


def per_device(cotangent, token_ids, block_counts, block_slot, table, m_code, m_scale, v_code, v_scale):
    del block_counts
    n_dp, n_mp = lax.axis_size("dp"), lax.axis_size("mp")
    n_tok, width = cotangent.shape
    rows = table.shape[0]
    full = width // LANES * LANES + LANES
    bf, f32, i32 = jnp.bfloat16, jnp.float32, jnp.int32
    wide, line = (width, rows), (1, rows)
    outs = pl.pallas_call(
        functools.partial(kernel, n_dp, n_mp),
        out_shape=(
            jax.ShapeDtypeStruct(wide, bf),
            jax.ShapeDtypeStruct(wide, bf),
            jax.ShapeDtypeStruct(line, f32),
            jax.ShapeDtypeStruct(wide, bf),
            jax.ShapeDtypeStruct(line, f32),
        ),
        in_specs=[pl.BlockSpec(memory_space=pltpu.HBM)] * 8,
        out_specs=[pl.BlockSpec(memory_space=pltpu.HBM)] * 5,
        scratch_shapes=[
            pltpu.VMEM((width, n_tok), bf),
            pltpu.VMEM((1, n_tok), i32),
            pltpu.VMEM((1, block_slot.shape[0]), i32),
            pltpu.VMEM(wide, bf),
            pltpu.VMEM(wide, bf),
            pltpu.VMEM(line, f32),
            pltpu.VMEM(wide, bf),
            pltpu.VMEM(line, f32),
            pltpu.VMEM((n_dp, CAP, full), bf),
            pltpu.VMEM((n_dp, CAP, full), bf),
            pltpu.VMEM(wide, f32),
            pltpu.VMEM(wide, f32),
            pltpu.VMEM((2, rows), f32),
            pltpu.VMEM((n_mp, 2, rows), f32),
            pltpu.VMEM(wide, bf),
            pltpu.VMEM(wide, bf),
            pltpu.VMEM(wide, bf),
            pltpu.VMEM(line, f32),
            pltpu.VMEM(line, f32),
            pltpu.SemaphoreType.DMA((8,)),
            pltpu.SemaphoreType.DMA((5,)),
            pltpu.SemaphoreType.DMA,
            pltpu.SemaphoreType.DMA,
            pltpu.SemaphoreType.DMA,
            pltpu.SemaphoreType.DMA,
        ],
        compiler_params=pltpu.CompilerParams(
            collective_id=0, has_side_effects=True, vmem_limit_bytes=63 * 1024 * 1024
        ),
        name="embed_adam",
    )(
        cotangent.T, token_ids.reshape(1, -1), block_slot.reshape(1, -1), table.T,
        m_code.T, m_scale.reshape(line), v_code.T, v_scale.reshape(line),
    )
    new_table, new_m_code, new_m_scale, new_v_code, new_v_scale = outs
    return (new_table.T, new_m_code.T, new_m_scale.reshape(rows), new_v_code.T, new_v_scale.reshape(rows))


def solution(mesh):
    return jax.shard_map(
        per_device,
        mesh=mesh,
        in_specs=(
            P("dp", "mp"),
            P("dp"),
            P("dp", None),
            P(),
            P("dp", "mp"),
            P("dp", "mp"),
            P("dp"),
            P("dp", "mp"),
            P("dp"),
        ),
        out_specs=(P("dp", "mp"), P("dp", "mp"), P("dp"), P("dp", "mp"), P("dp")),
        check_vma=False,
    )
```

```python
import functools
import math

import jax
import jax.numpy as jnp
from jax import lax
from jax.experimental import pallas as pl
from jax.experimental.pallas import tpu as pltpu
from jax.sharding import PartitionSpec as P

BLOCK = 256
CAP = 8
LANES = 128
MESH = pl.DeviceIdType.MESH

beta_first = 0.9
beta_second = 0.95
step_rate = 0.05
eps_root = 1e-08
eps_peak = 1e-06


def fold(i, side):
    half = side // 2
    return jnp.where(i < half, i, side + half - 1 - i)


def dp_rank(d, n):
    side = math.isqrt(n)
    return (d % side) * side + fold(d // side, side)


def dp_at(r, n):
    side = math.isqrt(n)
    return fold(r % side, side) * side + r // side


def exchange(
    n_dp, n_mp,
    cot_hbm, tok_hbm, slot_hbm, tab_hbm, mc_hbm, ms_hbm, vc_hbm, vs_hbm,
    nt, mom, sec, top,
    cot, tok, slot, tab, mc, ms, vc, vs,
    send, recv, peak, peaks,
    in_sems, send_sem, recv_sem, psend_sem, precv_sem, ready, go, mp_in, mp_go,
):
    dp, mp = lax.axis_index("dp"), lax.axis_index("mp")
    side = math.isqrt(n_dp)
    r_dp = dp_rank(dp, n_dp)
    level, place_in = r_dp // side, r_dp % side
    hub = level == 0
    not_hub = level > 0
    known = jnp.where(hub, 0, jnp.maximum(level - 2, 1))
    later = jnp.where(hub, 1, level + 3)
    width, n_tok = cot.shape
    rows = tab.shape[1]
    n_blk = slot.shape[1]
    n_slot = n_dp * CAP
    full = send.shape[2]
    n_meta = full - width
    strip = 48 if width % 48 == 0 else 16

    barrier = pltpu.get_barrier_semaphore()
    copies = [
        pltpu.make_async_copy(src, dst, in_sems.at[i])
        for i, (src, dst) in enumerate(
            ((tok_hbm, tok), (slot_hbm, slot), (cot_hbm, cot), (ms_hbm, ms), (vs_hbm, vs), (mc_hbm, mc), (vc_hbm, vc), (tab_hbm, tab))
        )
    ]
    for copy in copies:
        copy.start()

    def signal(sem, axis, to):
        pl.semaphore_signal(sem, inc=1, device_id={axis: to}, device_id_type=MESH)

    def over_levels(low, high, fn):
        def body(k, _):
            for i in range(side):
                fn(k * side + i)
            return 0

        lax.fori_loop(low, high, body, 0)

    def over_others(fn):
        for i in range(1, side):
            fn(level * side + lax.rem(place_in + i, side))

    def over_mp(fn):
        for i in range(1, n_mp):
            fn(lax.rem(mp + i, n_mp))

    @pl.when(hub)
    def _():
        over_others(lambda r: signal(barrier, "dp", dp_at(r, n_dp)))
        over_mp(lambda m: signal(barrier, "mp", m))

    over_levels(later, side, lambda r: signal(barrier, "dp", dp_at(r, n_dp)))
    pl.semaphore_wait(barrier, jnp.where(hub, side + n_mp - 2, known * side))
    over_levels(0, known, lambda r: signal(ready.at[r_dp], "dp", dp_at(r, n_dp)))

    copies[0].wait()
    copies[1].wait()
    ids = tok[...]
    low = ids % BLOCK
    blk = ids // BLOCK
    in_block = (lax.broadcasted_iota(jnp.int32, (n_blk, n_tok), 0) == blk).astype(jnp.bfloat16)
    slot_rows = jnp.broadcast_to(slot[...].astype(jnp.float32), (16, n_blk)).astype(jnp.bfloat16)
    held = jnp.dot(slot_rows, in_block, preferred_element_type=jnp.float32)[0:1, :].astype(jnp.int32)
    owner = held // 2
    sub = held % 2
    of_owner = (lax.broadcasted_iota(jnp.int32, (n_dp, n_tok), 0) == owner).astype(jnp.float32)
    earlier = (
        lax.broadcasted_iota(jnp.int32, (n_tok, n_tok), 0) < lax.broadcasted_iota(jnp.int32, (n_tok, n_tok), 1)
    ).astype(jnp.bfloat16)
    before = jnp.dot(of_owner.astype(jnp.bfloat16), earlier, preferred_element_type=jnp.float32)
    rank = jnp.sum(of_owner * before, axis=0, keepdims=True)
    place = owner * CAP + rank.astype(jnp.int32)
    chosen = (lax.broadcasted_iota(jnp.int32, (n_slot, n_tok), 0) == place).astype(jnp.bfloat16)

    meta_row = lax.broadcasted_iota(jnp.int32, (n_meta, n_tok), 0)
    meta = jnp.where(meta_row == 0, low, jnp.where(meta_row == 1, (sub + 1) * BLOCK, 0))
    meta = meta.astype(jnp.float32).astype(jnp.bfloat16)
    copies[2].wait()
    tokens = jnp.concatenate([cot[...], meta], axis=0)
    sent = lax.dot_general(chosen, tokens, (((1,), (1,)), ((), ())), preferred_element_type=jnp.float32)
    send[...] = sent.reshape(n_dp, CAP, full).astype(jnp.bfloat16)


    def rows_to(r):
        to = dp_at(r, n_dp)
        return pltpu.make_async_remote_copy(
            src_ref=send.at[to], dst_ref=recv.at[dp], send_sem=send_sem, recv_sem=recv_sem,
            device_id={"dp": to}, device_id_type=MESH,
        )

    def send_to(r):
        rows_to(r).start()

    over_levels(0, known, send_to)
    recv[pl.ds(dp, 1)] = send[pl.ds(dp, 1)]

    for copy in copies[3:]:
        copy.wait()
    for c in range(0, width, strip):
        at = pl.ds(c, strip)
        mom[at, :] = beta_first * (mc[at, :].astype(jnp.float32) * ms[...])
        sec[at, :] = beta_second * (vc[at, :].astype(jnp.float32) * vs[...])

    @pl.when(not_hub)
    def _():
        pl.semaphore_wait(go.at[0], 1)

    over_levels(known, jnp.where(hub, 0, level), send_to)
    over_others(send_to)

    for i in (1, 2):

        @pl.when(jnp.logical_and(not_hub, level + i < side))
        def _():
            pl.semaphore_wait(go.at[i], 1)
            for j in range(side):
                send_to((level + i) * side + j)

    def next_level(k, _):
        for i in range(side):
            pl.semaphore_wait(ready.at[k * side + i], 1)
            send_to(k * side + i)

        @pl.when(hub)
        def _():
            for i in range(3):

                @pl.when(k > i)
                def _():
                    signal(go.at[i], "dp", dp_at((k - i) * side + place_in, n_dp))

            over_mp(lambda m: signal(mp_in.at[k], "mp", m))

        return 0

    lax.fori_loop(later, side, next_level, 0)
    others = pl.ds(0, n_dp - 1)
    pltpu.make_async_copy(recv.at[others], recv.at[others], recv_sem).wait()

    got = recv[...].astype(jnp.float32).reshape(n_slot, full).astype(jnp.bfloat16)
    last = full - LANES
    pick = (lax.broadcasted_iota(jnp.int32, (LANES, rows), 0) >= width - last).astype(jnp.bfloat16)
    index = jnp.dot(got[:, last:full], pick, preferred_element_type=jnp.float32).astype(jnp.int32)
    row = lax.broadcasted_iota(jnp.int32, (n_slot, rows), 1) + BLOCK
    selector = (row == index).astype(jnp.bfloat16)
    grad = lax.dot_general(got, selector, (((0,), (0,)), ((), ())), preferred_element_type=jnp.float32)

    m_top = jnp.zeros((8, rows), jnp.float32)
    v_top = jnp.zeros((8, rows), jnp.float32)
    for c in range(0, width, strip):
        at = pl.ds(c, strip)
        g = grad[c : c + strip]
        moment = mom[at, :] + 0.1 * g
        second = sec[at, :] + 0.05 * (g * g)
        mom[at, :] = moment
        sec[at, :] = second
        m_top = jnp.maximum(m_top, jnp.max(jnp.abs(moment).reshape(strip // 8, 8, rows), axis=0))
        v_top = jnp.maximum(v_top, jnp.max(second.reshape(strip // 8, 8, rows), axis=0))
    peak[0:1, :] = jnp.max(m_top, axis=0, keepdims=True)
    peak[1:2, :] = jnp.max(v_top, axis=0, keepdims=True)

    @pl.when(not_hub)
    def _():
        pl.semaphore_wait(mp_go, 1)

    def send_peak(to):
        pltpu.make_async_remote_copy(
            src_ref=peak, dst_ref=peaks.at[mp], send_sem=psend_sem, recv_sem=precv_sem,
            device_id={"mp": to}, device_id_type=MESH,
        ).start()

    over_mp(send_peak)
    peaks[pl.ds(mp, 1)] = peak[...][None]

    for c in range(0, width, strip):
        at = pl.ds(c, strip)
        moment, second = mom[at, :], sec[at, :]
        nt[at, :] = (tab[at, :].astype(jnp.float32) - step_rate * (moment / (jnp.sqrt(second) + eps_root))).astype(jnp.bfloat16)

    def mp_level(k, _):
        pl.semaphore_wait(mp_in.at[k], n_mp - 1)
        signal(mp_go, "dp", dp_at(k * side + place_in, n_dp))
        return 0

    lax.fori_loop(1, jnp.where(hub, side, 1), mp_level, 0)
    pltpu.make_async_copy(send.at[others], send.at[others], send_sem).wait()
    others = pl.ds(0, n_mp - 1)
    pltpu.make_async_copy(peaks.at[others], peaks.at[others], precv_sem).wait()
    top[...] = jnp.max(peaks[...], axis=0)
    pltpu.make_async_copy(peaks.at[others], peaks.at[others], psend_sem).wait()


def write(
    nt, mom, sec, top,
    nt_hbm, nm_hbm, nms_hbm, nv_hbm, nvs_hbm,
    nm, nv, nms, nvs, sems,
):
    width = nt.shape[0]
    strip = 112 if width % 112 == 0 else 16
    m_peak, v_peak = top[0:1], top[1:2]
    nms[...] = m_peak
    nvs[...] = v_peak
    outs = [pltpu.make_async_copy(nt, nt_hbm, sems.at[0]), pltpu.make_async_copy(nms, nms_hbm, sems.at[1]), pltpu.make_async_copy(nvs, nvs_hbm, sems.at[2])]
    for out in outs:
        out.start()
    m_peak, v_peak = m_peak + eps_peak, v_peak + eps_peak
    for i, c in enumerate(range(0, width, strip)):
        at = pl.ds(c, strip)
        nm[at, :] = (mom[at, :] / m_peak).astype(jnp.bfloat16)
        nv[at, :] = (sec[at, :] / v_peak).astype(jnp.bfloat16)
        for j, (src, dst) in enumerate(((nm, nm_hbm), (nv, nv_hbm))):
            outs.append(pltpu.make_async_copy(src.at[at], dst.at[at], sems.at[3 + 2 * i + j]))
            outs[-1].start()
    for out in outs:
        out.wait()


def per_device(cotangent, token_ids, block_counts, block_slot, table, m_code, m_scale, v_code, v_scale):
    del block_counts
    n_dp, n_mp = lax.axis_size("dp"), lax.axis_size("mp")
    n_tok, width = cotangent.shape
    rows = table.shape[0]
    full = width // LANES * LANES + LANES
    bf, f32, i32 = jnp.bfloat16, jnp.float32, jnp.int32
    wide, line = (width, rows), (1, rows)
    hbm = pl.BlockSpec(memory_space=pltpu.HBM)
    vmem = pl.BlockSpec(memory_space=pltpu.VMEM)
    operands = (
        cotangent.T, token_ids.reshape(1, -1), block_slot.reshape(1, -1), table.T,
        m_code.T, m_scale.reshape(line), v_code.T, v_scale.reshape(line),
    )
    operands = [pltpu.with_memory_space_constraint(x, pltpu.HBM) for x in operands]
    held = pl.pallas_call(
        functools.partial(exchange, n_dp, n_mp),
        out_shape=(pltpu.VMEM(wide, bf), pltpu.VMEM(wide, f32), pltpu.VMEM(wide, f32), pltpu.VMEM((2, rows), f32)),
        in_specs=[hbm] * 8,
        out_specs=[vmem] * 4,
        scratch_shapes=[
            pltpu.VMEM((width, n_tok), bf),
            pltpu.VMEM((1, n_tok), i32),
            pltpu.VMEM((1, block_slot.shape[0]), i32),
            pltpu.VMEM(wide, bf),
            pltpu.VMEM(wide, bf),
            pltpu.VMEM(line, f32),
            pltpu.VMEM(wide, bf),
            pltpu.VMEM(line, f32),
            pltpu.VMEM((n_dp, CAP, full), bf),
            pltpu.VMEM((n_dp, CAP, full), bf),
            pltpu.VMEM((2, rows), f32),
            pltpu.VMEM((n_mp, 2, rows), f32),
            pltpu.SemaphoreType.DMA((8,)),
            pltpu.SemaphoreType.DMA,
            pltpu.SemaphoreType.DMA,
            pltpu.SemaphoreType.DMA,
            pltpu.SemaphoreType.DMA,
            pltpu.SemaphoreType.REGULAR((n_dp,)),
            pltpu.SemaphoreType.REGULAR((3,)),
            pltpu.SemaphoreType.REGULAR((math.isqrt(n_dp),)),
            pltpu.SemaphoreType.REGULAR,
        ],
        compiler_params=pltpu.CompilerParams(
            collective_id=0, has_side_effects=True, vmem_limit_bytes=32 * 1024 * 1024
        ),
        name="embed_adam",
    )(*operands)
    new_table, new_m_code, new_m_scale, new_v_code, new_v_scale = pl.pallas_call(
        write,
        out_shape=(
            jax.ShapeDtypeStruct(wide, bf),
            jax.ShapeDtypeStruct(wide, bf),
            jax.ShapeDtypeStruct(line, f32),
            jax.ShapeDtypeStruct(wide, bf),
            jax.ShapeDtypeStruct(line, f32),
        ),
        in_specs=[vmem] * 4,
        out_specs=[hbm] * 5,
        scratch_shapes=[
            pltpu.VMEM(wide, bf),
            pltpu.VMEM(wide, bf),
            pltpu.VMEM(line, f32),
            pltpu.VMEM(line, f32),
            pltpu.SemaphoreType.DMA((64,)),
        ],
        compiler_params=pltpu.CompilerParams(vmem_limit_bytes=16 * 1024 * 1024),
        name="codes",
    )(*held)
    return (new_table.T, new_m_code.T, new_m_scale.reshape(rows), new_v_code.T, new_v_scale.reshape(rows))


def solution(mesh):
    return jax.shard_map(
        per_device,
        mesh=mesh,
        in_specs=(
            P("dp", "mp"),
            P("dp"),
            P("dp", None),
            P(),
            P("dp", "mp"),
            P("dp", "mp"),
            P("dp"),
            P("dp", "mp"),
            P("dp"),
        ),
        out_specs=(P("dp", "mp"), P("dp", "mp"), P("dp"), P("dp", "mp"), P("dp")),
        check_vma=False,
    )
```

```python
import functools
import math

import jax
import jax.numpy as jnp
from jax import lax
from jax.experimental import pallas as pl
from jax.experimental.pallas import tpu as pltpu
from jax.sharding import PartitionSpec as P

BLOCK = 256
CAP = 8
LANES = 128
CUT = 6
MESH = pl.DeviceIdType.MESH

beta_first = 0.9
beta_second = 0.95
step_rate = 0.05
eps_root = 1e-08
eps_peak = 1e-06


def fold(i, side):
    half = side // 2
    return jnp.where(i < half, i, side + half - 1 - i)


def dp_rank(d, n):
    side = math.isqrt(n)
    return (d % side) * side + fold(d // side, side)


def dp_at(r, n):
    side = math.isqrt(n)
    return fold(r % side, side) * side + r // side


def exchange(
    n_dp, n_mp,
    cot_hbm, tok_hbm, slot_hbm, tab_hbm, mc_hbm, ms_hbm, vc_hbm, vs_hbm,
    nt, mom, sec, top,
    cot, tok, slot, scales, codes,
    send, recv, grad_acc, peak, peaks,
    in_sems, send_sem, recv_sems, psend_sem, precv_sem, ready, go, mp_in, mp_go,
):
    dp, mp = lax.axis_index("dp"), lax.axis_index("mp")
    side = math.isqrt(n_dp)
    r_dp = dp_rank(dp, n_dp)
    level, place_in = r_dp // side, r_dp % side
    hub = level == 0
    not_hub = level > 0
    n_early = side * CUT // 8 * side
    late = (r_dp >= n_early).astype(jnp.int32)
    known = jnp.where(hub, 0, jnp.maximum(level - 2, 1))
    later = jnp.where(hub, 1, level + 3)
    width, n_tok = cot.shape
    rows = codes.shape[2]
    ms, vs = scales.at[0], scales.at[1]
    mc, vc, tab = codes.at[0], codes.at[1], codes.at[2]
    n_blk = slot.shape[1]
    n_slot = n_dp * CAP
    full = send.shape[2]
    n_meta = full - width
    strip = 48 if width % 48 == 0 else 16

    barrier = pltpu.get_barrier_semaphore()
    copies = [
        pltpu.make_async_copy(src, dst, in_sems.at[i])
        for i, src, dst in (
            (0, tok_hbm, tok), (1, slot_hbm, slot), (2, cot_hbm, cot),
            (3, ms_hbm, ms), (3, vs_hbm, vs), (4, mc_hbm, mc), (4, vc_hbm, vc), (4, tab_hbm, tab),
        )
    ]
    for copy in copies:
        copy.start()

    def signal(sem, axis, to):
        pl.semaphore_signal(sem, inc=1, device_id={axis: to}, device_id_type=MESH)

    def over_levels(low, high, fn):
        def body(k, _):
            for i in range(side):
                fn(k * side + i)
            return 0

        lax.fori_loop(low, high, body, 0)

    def over_others(fn):
        for i in range(1, side):
            fn(level * side + lax.rem(place_in + i, side))

    def over_mp(fn):
        for i in range(1, n_mp):
            fn(lax.rem(mp + i, n_mp))

    @pl.when(hub)
    def _():
        over_others(lambda r: signal(barrier, "dp", dp_at(r, n_dp)))
        over_mp(lambda m: signal(barrier, "mp", m))

    @pl.when(not_hub)
    def _():
        signal(barrier, "mp", mp + 1 - 2 * lax.rem(mp, 2))

    over_levels(later, side, lambda r: signal(barrier, "dp", dp_at(r, n_dp)))
    pl.semaphore_wait(barrier, jnp.where(hub, side + n_mp - 2, known * side + 1))
    earlier = (
        lax.broadcasted_iota(jnp.int32, (n_tok, n_tok), 0) < lax.broadcasted_iota(jnp.int32, (n_tok, n_tok), 1)
    ).astype(jnp.bfloat16)
    copies[0].wait()
    copies[1].wait()
    ids = tok[...]
    low = ids % BLOCK
    blk = ids // BLOCK
    in_block = (lax.broadcasted_iota(jnp.int32, (n_blk, n_tok), 0) == blk).astype(jnp.bfloat16)
    slot_rows = jnp.broadcast_to(slot[...].astype(jnp.float32), (16, n_blk)).astype(jnp.bfloat16)
    held = jnp.dot(slot_rows, in_block, preferred_element_type=jnp.float32)[0:1, :].astype(jnp.int32)
    owner = held // 2
    sub = held % 2
    of_owner = (lax.broadcasted_iota(jnp.int32, (n_dp, n_tok), 0) == owner).astype(jnp.float32)
    before = jnp.dot(of_owner.astype(jnp.bfloat16), earlier, preferred_element_type=jnp.float32)
    rank = jnp.sum(of_owner * before, axis=0, keepdims=True)
    place = owner * CAP + rank.astype(jnp.int32)
    chosen = (lax.broadcasted_iota(jnp.int32, (n_slot, n_tok), 0) == place).astype(jnp.bfloat16)

    meta_row = lax.broadcasted_iota(jnp.int32, (n_meta, n_tok), 0)
    meta = jnp.where(meta_row == 0, low, jnp.where(meta_row == 1, (sub + 1) * BLOCK, 0))
    meta = meta.astype(jnp.float32).astype(jnp.bfloat16)
    copies[2].wait()
    tokens = jnp.concatenate([cot[...], meta], axis=0)
    sent = lax.dot_general(chosen, tokens, (((1,), (1,)), ((), ())), preferred_element_type=jnp.float32)
    send[...] = sent.reshape(n_dp, CAP, full).astype(jnp.bfloat16)


    def rows_to(r):
        to = dp_at(r, n_dp)
        return pltpu.make_async_remote_copy(
            src_ref=send.at[to], dst_ref=recv.at[r_dp], send_sem=send_sem, recv_sem=recv_sems.at[late],
            device_id={"dp": to}, device_id_type=MESH,
        )

    def send_to(r):
        rows_to(r).start()

    over_levels(0, jnp.minimum(known, 1), send_to)
    over_levels(0, known, lambda r: signal(ready.at[level], "dp", dp_at(r, n_dp)))
    recv[pl.ds(r_dp, 1)] = send[pl.ds(dp, 1)]

    pltpu.make_async_copy(scales, scales, in_sems.at[3]).wait()
    pltpu.make_async_copy(codes, codes, in_sems.at[4]).wait()
    for c in range(0, width, strip):
        at = pl.ds(c, strip)
        mom[at, :] = beta_first * (mc[at, :].astype(jnp.float32) * ms[...])
        sec[at, :] = beta_second * (vc[at, :].astype(jnp.float32) * vs[...])

    over_levels(1, known, send_to)
    @pl.when(not_hub)
    def _():
        pl.semaphore_wait(go.at[0], 1)

    over_levels(known, jnp.where(hub, 0, level), send_to)
    over_others(send_to)

    for i in (1, 2):

        @pl.when(jnp.logical_and(not_hub, level + i < side))
        def _():
            pl.semaphore_wait(go.at[i], 1)
            for j in range(side):
                send_to((level + i) * side + j)

    def next_level(k, _):
        pl.semaphore_wait(ready.at[k], side)
        for i in range(side):
            send_to(k * side + i)

        @pl.when(hub)
        def _():
            for i in range(3):

                @pl.when(k > i)
                def _():
                    signal(go.at[i], "dp", dp_at((k - i) * side + place_in, n_dp))

            over_mp(lambda m: signal(mp_in, "mp", m))

        return 0

    lax.fori_loop(later, side, next_level, 0)
    others = pl.ds(0, n_dp - 1)
    last = full - LANES
    pick = (lax.broadcasted_iota(jnp.int32, (LANES, rows), 0) >= width - last).astype(jnp.bfloat16)

    def wait_rows(part, n):
        @pl.when(late == part)
        def _():
            pltpu.make_async_copy(recv.at[pl.ds(0, n - 1)], recv.at[pl.ds(0, n - 1)], recv_sems.at[part]).wait()

        @pl.when(late != part)
        def _():
            pltpu.make_async_copy(recv.at[pl.ds(0, n)], recv.at[pl.ds(0, n)], recv_sems.at[part]).wait()

    def sum_rows(first, n):
        got = recv[first : first + n].astype(jnp.float32).reshape(n * CAP, full).astype(jnp.bfloat16)
        index = jnp.dot(got[:, last:full], pick, preferred_element_type=jnp.float32).astype(jnp.int32)
        row = lax.broadcasted_iota(jnp.int32, (n * CAP, rows), 1) + BLOCK
        selector = (row == index).astype(jnp.bfloat16)
        return lax.dot_general(got, selector, (((0,), (0,)), ((), ())), preferred_element_type=jnp.float32)

    wait_rows(0, n_early)
    grad_acc[...] = sum_rows(0, n_early)
    wait_rows(1, n_dp - n_early)
    grad = sum_rows(n_early, n_dp - n_early)

    m_top = jnp.zeros((8, rows), jnp.float32)
    v_top = jnp.zeros((8, rows), jnp.float32)
    for c in range(0, width, strip):
        at = pl.ds(c, strip)
        g = grad_acc[at, :] + grad[c : c + strip]
        moment = mom[at, :] + 0.1 * g
        second = sec[at, :] + 0.05 * (g * g)
        mom[at, :] = moment
        sec[at, :] = second
        m_top = jnp.maximum(m_top, jnp.max(jnp.abs(moment).reshape(strip // 8, 8, rows), axis=0))
        v_top = jnp.maximum(v_top, jnp.max(second.reshape(strip // 8, 8, rows), axis=0))
    peak[0:1, :] = jnp.max(m_top, axis=0, keepdims=True)
    peak[1:2, :] = jnp.max(v_top, axis=0, keepdims=True)

    @pl.when(not_hub)
    def _():
        pl.semaphore_wait(mp_go, 1)

    def send_peak(to):
        pltpu.make_async_remote_copy(
            src_ref=peak, dst_ref=peaks.at[mp], send_sem=psend_sem, recv_sem=precv_sem,
            device_id={"mp": to}, device_id_type=MESH,
        ).start()

    chips = n_mp // 2
    for i in sorted(range(chips), key=lambda i: -min(i, chips - i)):
        for core in (0, 1):
            if i or core:
                send_peak(lax.rem(mp // 2 + i, chips) * 2 + lax.rem(mp + core, 2))
    peaks[pl.ds(mp, 1)] = peak[...][None]

    for c in range(0, width, strip):
        at = pl.ds(c, strip)
        moment, second = mom[at, :], sec[at, :]
        nt[at, :] = (tab[at, :].astype(jnp.float32) - step_rate * (moment / (jnp.sqrt(second) + eps_root))).astype(jnp.bfloat16)

    @pl.when(hub)
    def _():
        pl.semaphore_wait(mp_in, (n_mp - 1) * (side - 1))
        for k in range(1, side):
            signal(mp_go, "dp", dp_at(k * side + place_in, n_dp))

    pltpu.make_async_copy(send.at[others], send.at[others], send_sem).wait()
    others = pl.ds(0, n_mp - 1)
    pltpu.make_async_copy(peaks.at[others], peaks.at[others], precv_sem).wait()
    top[...] = jnp.max(peaks[...], axis=0)
    pltpu.make_async_copy(peaks.at[others], peaks.at[others], psend_sem).wait()


def strips(width):
    strip = 112 if width % 112 == 0 else 16
    return [pl.ds(c, strip) for c in range(0, width, strip)]


def write(
    nt, mom, sec, top,
    nt_hbm, nm_hbm, nms_hbm, nv_hbm, nvs_hbm,
    nm, nv, nms, nvs, sems,
):
    width = nt.shape[0]
    m_peak, v_peak = top[0:1], top[1:2]
    nms[...] = m_peak
    nvs[...] = v_peak
    outs = [pltpu.make_async_copy(nt, nt_hbm, sems.at[0]), pltpu.make_async_copy(nms, nms_hbm, sems.at[1]), pltpu.make_async_copy(nvs, nvs_hbm, sems.at[2])]
    for out in outs:
        out.start()
    m_peak, v_peak = m_peak + eps_peak, v_peak + eps_peak
    for i, at in enumerate(strips(width)):
        nm[at, :] = (mom[at, :] / m_peak).astype(jnp.bfloat16)
        nv[at, :] = (sec[at, :] / v_peak).astype(jnp.bfloat16)
        for j, (src, dst) in enumerate(((nm, nm_hbm), (nv, nv_hbm))):
            outs.append(pltpu.make_async_copy(src.at[at], dst.at[at], sems.at[3 + 2 * i + j]))
            outs[-1].start()
    for out in outs:
        out.wait()


def per_device(cotangent, token_ids, block_counts, block_slot, table, m_code, m_scale, v_code, v_scale):
    del block_counts
    n_dp, n_mp = lax.axis_size("dp"), lax.axis_size("mp")
    n_tok, width = cotangent.shape
    rows = table.shape[0]
    full = width // LANES * LANES + LANES
    bf, f32, i32 = jnp.bfloat16, jnp.float32, jnp.int32
    wide, line = (width, rows), (1, rows)
    side = math.isqrt(n_dp)
    hbm = pl.BlockSpec(memory_space=pltpu.HBM)
    vmem = pl.BlockSpec(memory_space=pltpu.VMEM)
    operands = (
        cotangent.T, token_ids.reshape(1, -1), block_slot.reshape(1, -1), table.T,
        m_code.T, m_scale.reshape(line), v_code.T, v_scale.reshape(line),
    )
    operands = [pltpu.with_memory_space_constraint(x, pltpu.HBM) for x in operands]
    held = pl.pallas_call(
        functools.partial(exchange, n_dp, n_mp),
        out_shape=(pltpu.VMEM(wide, bf), pltpu.VMEM(wide, f32), pltpu.VMEM(wide, f32), pltpu.VMEM((2, rows), f32)),
        in_specs=[hbm] * 8,
        out_specs=[vmem] * 4,
        scratch_shapes=[
            pltpu.VMEM((width, n_tok), bf),
            pltpu.VMEM((1, n_tok), i32),
            pltpu.VMEM((1, block_slot.shape[0]), i32),
            pltpu.VMEM((2, 1, rows), f32),
            pltpu.VMEM((3, *wide), bf),
            pltpu.VMEM((n_dp, CAP, full), bf),
            pltpu.VMEM((n_dp, CAP, full), bf),
            pltpu.VMEM((full, rows), f32),
            pltpu.VMEM((2, rows), f32),
            pltpu.VMEM((n_mp, 2, rows), f32),
            pltpu.SemaphoreType.DMA((5,)),
            pltpu.SemaphoreType.DMA,
            pltpu.SemaphoreType.DMA((2,)),
            pltpu.SemaphoreType.DMA,
            pltpu.SemaphoreType.DMA,
            pltpu.SemaphoreType.REGULAR((side,)),
            pltpu.SemaphoreType.REGULAR((3,)),
            pltpu.SemaphoreType.REGULAR,
            pltpu.SemaphoreType.REGULAR,
        ],
        compiler_params=pltpu.CompilerParams(
            collective_id=0, has_side_effects=True, vmem_limit_bytes=32 * 1024 * 1024
        ),
        name="embed_adam",
    )(*operands)
    new_table, new_m_code, new_m_scale, new_v_code, new_v_scale = pl.pallas_call(
        write,
        out_shape=(
            jax.ShapeDtypeStruct(wide, bf),
            jax.ShapeDtypeStruct(wide, bf),
            jax.ShapeDtypeStruct(line, f32),
            jax.ShapeDtypeStruct(wide, bf),
            jax.ShapeDtypeStruct(line, f32),
        ),
        in_specs=[vmem] * 4,
        out_specs=[hbm] * 5,
        scratch_shapes=[
            pltpu.VMEM(wide, bf),
            pltpu.VMEM(wide, bf),
            pltpu.VMEM(line, f32),
            pltpu.VMEM(line, f32),
            pltpu.SemaphoreType.DMA((3 + 2 * len(strips(width)),)),
        ],
        compiler_params=pltpu.CompilerParams(vmem_limit_bytes=16 * 1024 * 1024),
        name="codes",
    )(*held)
    return (new_table.T, new_m_code.T, new_m_scale.reshape(rows), new_v_code.T, new_v_scale.reshape(rows))


def solution(mesh):
    return jax.shard_map(
        per_device,
        mesh=mesh,
        in_specs=(
            P("dp", "mp"),
            P("dp"),
            P("dp", None),
            P(),
            P("dp", "mp"),
            P("dp", "mp"),
            P("dp"),
            P("dp", "mp"),
            P("dp"),
        ),
        out_specs=(P("dp", "mp"), P("dp", "mp"), P("dp"), P("dp", "mp"), P("dp")),
        check_vma=False,
    )
```

```python
import functools
import math

import jax
import jax.numpy as jnp
from jax import lax
from jax.experimental import pallas as pl
from jax.experimental.pallas import tpu as pltpu
from jax.sharding import PartitionSpec as P

BLOCK = 256
CAP = 8
LANES = 128
CUT = 7
MESH = pl.DeviceIdType.MESH

beta_first = 0.9
beta_second = 0.95
step_rate = 0.05
eps_root = 1e-08
eps_peak = 1e-06


def fold(i, side):
    half = side // 2
    return jnp.where(i < half, i, side + half - 1 - i)


def dp_rank(d, n):
    side = math.isqrt(n)
    return (d % side) * side + fold(d // side, side)


def dp_at(r, n):
    side = math.isqrt(n)
    return fold(r % side, side) * side + r // side


LATER = {8: (1, 4, 5, 8, 8, 8, 8, 8), 4: (1, 3, 4, 4), 2: (1, 2)}
SPREAD = max(later - level for table in LATER.values() for level, later in enumerate(table) if level)


def later_than(level, side):
    return sum(jnp.where(level == j, later, 0) for j, later in enumerate(LATER[side]))


def known_to(level, side):
    return sum(jnp.where(level >= later, 1, 0) for later in LATER[side])


def exchange(
    n_dp, n_mp,
    cot_hbm, tok_hbm, slot_hbm, tab_hbm, mc_hbm, ms_hbm, vc_hbm, vs_hbm,
    nt, mom, sec, top,
    cot, tok, slot, scales, codes,
    send, recv, grad_acc, peak, peaks,
    in_sems, send_sem, recv_sems, psend_sem, precv_sem, ready, mine, below, go, mp_in, mp_go, pal,
):
    dp, mp = lax.axis_index("dp"), lax.axis_index("mp")
    side = math.isqrt(n_dp)
    r_dp = dp_rank(dp, n_dp)
    level, place_in = r_dp // side, r_dp % side
    hub = level == 0
    middle = side // 2
    not_hub = level > 0
    n_early = side * CUT // 8 * side
    late = (r_dp >= n_early).astype(jnp.int32)
    known = known_to(level, side)
    later = later_than(level, side)
    width, n_tok = cot.shape
    rows = codes.shape[2]
    ms, vs = scales.at[0], scales.at[1]
    mc, vc, tab = codes.at[0], codes.at[1], codes.at[2]
    n_blk = slot.shape[1]
    n_slot = n_dp * CAP
    full = send.shape[2]
    n_meta = full - width
    strip = 48 if width % 48 == 0 else 16

    barrier = pltpu.get_barrier_semaphore()
    partner = mp + 1 - 2 * lax.rem(mp, 2)
    copies = [
        pltpu.make_async_copy(src, dst, in_sems.at[i])
        for i, src, dst in (
            (0, tok_hbm, tok), (1, slot_hbm, slot), (2, cot_hbm, cot),
            (3, ms_hbm, ms), (3, vs_hbm, vs), (4, mc_hbm, mc), (4, vc_hbm, vc), (4, tab_hbm, tab),
        )
    ]
    for copy in copies:
        copy.start()

    def signal(sem, axis, to):
        pl.semaphore_signal(sem, inc=1, device_id={axis: to}, device_id_type=MESH)

    def over_levels(low, high, fn):
        def body(k, _):
            for i in range(side):
                fn(k * side + i)
            return 0

        lax.fori_loop(low, high, body, 0)

    def over_others(fn):
        for i in range(1, side):
            fn(level * side + lax.rem(place_in + i, side))

    def over_mp(fn):
        for i in range(1, n_mp):
            fn(lax.rem(mp + i, n_mp))

    @pl.when(hub)
    def _():
        over_others(lambda r: signal(barrier, "dp", dp_at(r, n_dp)))
        over_mp(lambda m: signal(barrier, "mp", m))

    @pl.when(not_hub)
    def _():
        signal(barrier, "mp", partner)

    over_levels(later, side, lambda r: signal(barrier, "dp", dp_at(r, n_dp)))
    pl.semaphore_wait(barrier, jnp.where(hub, side + n_mp - 2, known * side + 1))
    @pl.when(not_hub)
    def _():
        signal(mine.at[level], "dp", dp_at(place_in, n_dp))

    over_levels(0, known, lambda r: signal(ready.at[level], "dp", dp_at(r, n_dp)))

    earlier = (
        lax.broadcasted_iota(jnp.int32, (n_tok, n_tok), 0) < lax.broadcasted_iota(jnp.int32, (n_tok, n_tok), 1)
    ).astype(jnp.bfloat16)
    copies[0].wait()
    copies[1].wait()
    ids = tok[...]
    low = ids % BLOCK
    blk = ids // BLOCK
    in_block = (lax.broadcasted_iota(jnp.int32, (n_blk, n_tok), 0) == blk).astype(jnp.bfloat16)
    slot_rows = jnp.broadcast_to(slot[...].astype(jnp.float32), (16, n_blk)).astype(jnp.bfloat16)
    held = jnp.dot(slot_rows, in_block, preferred_element_type=jnp.float32)[0:1, :].astype(jnp.int32)
    owner = held // 2
    sub = held % 2
    of_owner = (lax.broadcasted_iota(jnp.int32, (n_dp, n_tok), 0) == owner).astype(jnp.float32)
    before = jnp.dot(of_owner.astype(jnp.bfloat16), earlier, preferred_element_type=jnp.float32)
    rank = jnp.sum(of_owner * before, axis=0, keepdims=True)
    place = dp_rank(owner, n_dp) * CAP + rank.astype(jnp.int32)

    meta_row = lax.broadcasted_iota(jnp.int32, (n_meta, n_tok), 0)
    meta = jnp.where(meta_row == 0, low, jnp.where(meta_row == 1, (sub + 1) * BLOCK, 0))
    meta = meta.astype(jnp.float32).astype(jnp.bfloat16)
    copies[2].wait()
    tokens = jnp.concatenate([cot[...], meta], axis=0)

    def fill(first, n):
        slots = lax.broadcasted_iota(jnp.int32, (n * CAP, n_tok), 0) + first * CAP
        chosen = (slots == place).astype(jnp.bfloat16)
        rows_sent = lax.dot_general(chosen, tokens, (((1,), (1,)), ((), ())), preferred_element_type=jnp.float32)
        send[first : first + n] = rows_sent.reshape(n, CAP, full).astype(jnp.bfloat16)

    fill(0, side)

    def rows_to(r):
        to = dp_at(r, n_dp)
        return pltpu.make_async_remote_copy(
            src_ref=send.at[r], dst_ref=recv.at[r_dp], send_sem=send_sem, recv_sem=recv_sems.at[late],
            device_id={"dp": to}, device_id_type=MESH,
        )

    def send_to(r):
        rows_to(r).start()

    over_levels(0, jnp.minimum(known, 1), send_to)

    @pl.when(known > 1)
    def _():
        signal(pal, "mp", partner)

    fill(side, n_dp - side)
    recv[pl.ds(r_dp, 1)] = send[pl.ds(r_dp, 1)]

    pltpu.make_async_copy(scales, scales, in_sems.at[3]).wait()
    pltpu.make_async_copy(codes, codes, in_sems.at[4]).wait()
    for c in range(0, width, strip):
        at = pl.ds(c, strip)
        mom[at, :] = beta_first * (mc[at, :].astype(jnp.float32) * ms[...])
        sec[at, :] = beta_second * (vc[at, :].astype(jnp.float32) * vs[...])

    def known_level(k, _):
        pl.semaphore_wait(pal, 1)
        for i in range(side):
            send_to(k * side + i)

        @pl.when(k + 1 < known)
        def _():
            signal(pal, "mp", partner)

        return 0

    lax.fori_loop(1, known, known_level, 0)

    @pl.when(not_hub)
    def _():
        pl.semaphore_wait(below, 1)

    over_levels(known, jnp.where(hub, 0, jnp.minimum(level, middle)), send_to)
    @pl.when(not_hub)
    def _():
        pl.semaphore_wait(go.at[0], 1)

    over_levels(middle, level, send_to)
    over_others(send_to)

    for i in range(1, SPREAD):

        @pl.when(jnp.logical_and(not_hub, level + i < later))
        def _():
            pl.semaphore_wait(go.at[i], 1)
            for j in range(side):
                send_to((level + i) * side + j)

    def tell_below(k):
        pl.semaphore_wait(mine.at[k], 1)
        signal(below, "dp", dp_at(k * side + place_in, n_dp))

    def next_level(k, _):
        @pl.when(jnp.logical_and(hub, k <= middle))
        def _():
            tell_below(k)

        @pl.when(jnp.logical_and(hub, k == middle))
        def _():
            for j in range(middle + 1, side):
                tell_below(j)

        pl.semaphore_wait(ready.at[k], side)
        for i in range(side):
            send_to(k * side + i)

        @pl.when(hub)
        def _():
            for i in range(SPREAD):

                @pl.when(jnp.logical_and(k > i, k < later_than(k - i, side)))
                def _():
                    signal(go.at[i], "dp", dp_at((k - i) * side + place_in, n_dp))

            over_mp(lambda m: signal(mp_in, "mp", m))

        return 0

    lax.fori_loop(later, side, next_level, 0)
    others = pl.ds(0, n_dp - 1)
    last = full - LANES
    pick = (lax.broadcasted_iota(jnp.int32, (LANES, rows), 0) >= width - last).astype(jnp.bfloat16)

    def wait_rows(part, n):
        @pl.when(late == part)
        def _():
            pltpu.make_async_copy(recv.at[pl.ds(0, n - 1)], recv.at[pl.ds(0, n - 1)], recv_sems.at[part]).wait()

        @pl.when(late != part)
        def _():
            pltpu.make_async_copy(recv.at[pl.ds(0, n)], recv.at[pl.ds(0, n)], recv_sems.at[part]).wait()

    def sum_rows(first, n):
        got = recv[first : first + n].astype(jnp.float32).reshape(n * CAP, full).astype(jnp.bfloat16)
        index = jnp.dot(got[:, last:full], pick, preferred_element_type=jnp.float32).astype(jnp.int32)
        row = lax.broadcasted_iota(jnp.int32, (n * CAP, rows), 1) + BLOCK
        selector = (row == index).astype(jnp.bfloat16)
        return lax.dot_general(got, selector, (((0,), (0,)), ((), ())), preferred_element_type=jnp.float32)

    wait_rows(0, n_early)
    grad_acc[...] = sum_rows(0, n_early)
    wait_rows(1, n_dp - n_early)
    grad = sum_rows(n_early, n_dp - n_early)

    m_top = jnp.zeros((8, rows), jnp.float32)
    v_top = jnp.zeros((8, rows), jnp.float32)
    for c in range(0, width, strip):
        at = pl.ds(c, strip)
        g = grad_acc[at, :] + grad[c : c + strip]
        moment = mom[at, :] + 0.1 * g
        second = sec[at, :] + 0.05 * (g * g)
        mom[at, :] = moment
        sec[at, :] = second
        m_top = jnp.maximum(m_top, jnp.max(jnp.abs(moment).reshape(strip // 8, 8, rows), axis=0))
        v_top = jnp.maximum(v_top, jnp.max(second.reshape(strip // 8, 8, rows), axis=0))
    peak[0:1, :] = jnp.max(m_top, axis=0, keepdims=True)
    peak[1:2, :] = jnp.max(v_top, axis=0, keepdims=True)

    @pl.when(not_hub)
    def _():
        pl.semaphore_wait(mp_go, 1)

    def send_peak(to):
        pltpu.make_async_remote_copy(
            src_ref=peak, dst_ref=peaks.at[mp], send_sem=psend_sem, recv_sem=precv_sem,
            device_id={"mp": to}, device_id_type=MESH,
        ).start()

    chips = n_mp // 2
    for i in sorted(range(chips), key=lambda i: -min(i, chips - i)):
        for core in (0, 1):
            if i or core:
                send_peak(lax.rem(mp // 2 + i, chips) * 2 + lax.rem(mp + core, 2))
    peaks[pl.ds(mp, 1)] = peak[...][None]

    for c in range(0, width, strip):
        at = pl.ds(c, strip)
        moment, second = mom[at, :], sec[at, :]
        nt[at, :] = (tab[at, :].astype(jnp.float32) - step_rate * (moment / (jnp.sqrt(second) + eps_root))).astype(jnp.bfloat16)

    @pl.when(hub)
    def _():
        pl.semaphore_wait(mp_in, (n_mp - 1) * (side - 1))
        for k in range(1, side):
            signal(mp_go, "dp", dp_at(k * side + place_in, n_dp))

    pltpu.make_async_copy(send.at[others], send.at[others], send_sem).wait()
    others = pl.ds(0, n_mp - 1)
    pltpu.make_async_copy(peaks.at[others], peaks.at[others], precv_sem).wait()
    top[...] = jnp.max(peaks[...], axis=0)
    pltpu.make_async_copy(peaks.at[others], peaks.at[others], psend_sem).wait()


def strips(width):
    strip = 48 if width % 48 == 0 else 16
    return [pl.ds(c, strip) for c in range(0, width, strip)]


def write(
    nt, mom, sec, top,
    nt_hbm, nm_hbm, nms_hbm, nv_hbm, nvs_hbm,
    nm, nv, nms, nvs, sems,
):
    width = nt.shape[0]
    m_peak, v_peak = top[0:1], top[1:2]
    nms[...] = m_peak
    nvs[...] = v_peak
    parts = strips(width)

    def put(src, dst, sem, at):
        pltpu.make_async_copy(src.at[at], dst.at[at], sems.at[sem]).start()

    for at in parts:
        put(nt, nt_hbm, 0, at)
    lines = [pltpu.make_async_copy(nms, nms_hbm, sems.at[3]), pltpu.make_async_copy(nvs, nvs_hbm, sems.at[4])]
    for line in lines:
        line.start()
    m_peak, v_peak = m_peak + eps_peak, v_peak + eps_peak
    for at in parts:
        nm[at, :] = (mom[at, :] / m_peak).astype(jnp.bfloat16)
        put(nm, nm_hbm, 1, at)
        nv[at, :] = (sec[at, :] / v_peak).astype(jnp.bfloat16)
        put(nv, nv_hbm, 2, at)
    for i, (src, dst) in enumerate(((nt, nt_hbm), (nm, nm_hbm), (nv, nv_hbm))):
        pltpu.make_async_copy(src, dst, sems.at[i]).wait()
    for line in lines:
        line.wait()


def per_device(cotangent, token_ids, block_counts, block_slot, table, m_code, m_scale, v_code, v_scale):
    del block_counts
    n_dp, n_mp = lax.axis_size("dp"), lax.axis_size("mp")
    n_tok, width = cotangent.shape
    rows = table.shape[0]
    full = width // LANES * LANES + LANES
    bf, f32, i32 = jnp.bfloat16, jnp.float32, jnp.int32
    wide, line = (width, rows), (1, rows)
    side = math.isqrt(n_dp)
    hbm = pl.BlockSpec(memory_space=pltpu.HBM)
    vmem = pl.BlockSpec(memory_space=pltpu.VMEM)
    operands = (
        cotangent.T, token_ids.reshape(1, -1), block_slot.reshape(1, -1), table.T,
        m_code.T, m_scale.reshape(line), v_code.T, v_scale.reshape(line),
    )
    operands = [pltpu.with_memory_space_constraint(x, pltpu.HBM) for x in operands]
    held = pl.pallas_call(
        functools.partial(exchange, n_dp, n_mp),
        out_shape=(pltpu.VMEM(wide, bf), pltpu.VMEM(wide, f32), pltpu.VMEM(wide, f32), pltpu.VMEM((2, rows), f32)),
        in_specs=[hbm] * 8,
        out_specs=[vmem] * 4,
        scratch_shapes=[
            pltpu.VMEM((width, n_tok), bf),
            pltpu.VMEM((1, n_tok), i32),
            pltpu.VMEM((1, block_slot.shape[0]), i32),
            pltpu.VMEM((2, 1, rows), f32),
            pltpu.VMEM((3, *wide), bf),
            pltpu.VMEM((n_dp, CAP, full), bf),
            pltpu.VMEM((n_dp, CAP, full), bf),
            pltpu.VMEM((full, rows), f32),
            pltpu.VMEM((2, rows), f32),
            pltpu.VMEM((n_mp, 2, rows), f32),
            pltpu.SemaphoreType.DMA((5,)),
            pltpu.SemaphoreType.DMA,
            pltpu.SemaphoreType.DMA((2,)),
            pltpu.SemaphoreType.DMA,
            pltpu.SemaphoreType.DMA,
            pltpu.SemaphoreType.REGULAR((side,)),
            pltpu.SemaphoreType.REGULAR((side,)),
            pltpu.SemaphoreType.REGULAR,
            pltpu.SemaphoreType.REGULAR((SPREAD,)),
            pltpu.SemaphoreType.REGULAR,
            pltpu.SemaphoreType.REGULAR,
            pltpu.SemaphoreType.REGULAR,
        ],
        compiler_params=pltpu.CompilerParams(
            collective_id=0, has_side_effects=True, vmem_limit_bytes=32 * 1024 * 1024
        ),
        name="embed_adam",
    )(*operands)
    new_table, new_m_code, new_m_scale, new_v_code, new_v_scale = pl.pallas_call(
        write,
        out_shape=(
            jax.ShapeDtypeStruct(wide, bf),
            jax.ShapeDtypeStruct(wide, bf),
            jax.ShapeDtypeStruct(line, f32),
            jax.ShapeDtypeStruct(wide, bf),
            jax.ShapeDtypeStruct(line, f32),
        ),
        in_specs=[vmem] * 4,
        out_specs=[hbm] * 5,
        scratch_shapes=[
            pltpu.VMEM(wide, bf),
            pltpu.VMEM(wide, bf),
            pltpu.VMEM(line, f32),
            pltpu.VMEM(line, f32),
            pltpu.SemaphoreType.DMA((5,)),
        ],
        compiler_params=pltpu.CompilerParams(vmem_limit_bytes=16 * 1024 * 1024),
        name="codes",
    )(*held)
    return (new_table.T, new_m_code.T, new_m_scale.reshape(rows), new_v_code.T, new_v_scale.reshape(rows))


def solution(mesh):
    return jax.shard_map(
        per_device,
        mesh=mesh,
        in_specs=(
            P("dp", "mp"),
            P("dp"),
            P("dp", None),
            P(),
            P("dp", "mp"),
            P("dp", "mp"),
            P("dp"),
            P("dp", "mp"),
            P("dp"),
        ),
        out_specs=(P("dp", "mp"), P("dp", "mp"), P("dp"), P("dp", "mp"), P("dp")),
        check_vma=False,
    )
```

```python
import functools
import math

import jax
import jax.numpy as jnp
from jax import lax
from jax.experimental import pallas as pl
from jax.experimental.pallas import tpu as pltpu
from jax.sharding import PartitionSpec as P

BLOCK = 256
CAP = 8
LANES = 128
CUT = 7
MESH = pl.DeviceIdType.MESH

beta_first = 0.9
beta_second = 0.95
step_rate = 0.05
eps_root = 1e-08
eps_peak = 1e-06


def fold(i, side):
    half = side // 2
    return jnp.where(i < half, i, side + half - 1 - i)


def dp_rank(d, n):
    side = math.isqrt(n)
    return (d % side) * side + fold(d // side, side)


def dp_at(r, n):
    side = math.isqrt(n)
    return fold(r % side, side) * side + r // side


LATER = {8: (1, 4, 5, 8, 8, 8, 8, 8), 4: (1, 3, 4, 4), 2: (1, 2)}
SPREAD = max(later - level for table in LATER.values() for level, later in enumerate(table) if level)


def later_than(level, side):
    return sum(jnp.where(level == j, later, 0) for j, later in enumerate(LATER[side]))


def known_to(level, side):
    return sum(jnp.where(level >= later, 1, 0) for later in LATER[side])


def exchange(
    n_dp, n_mp,
    cot_hbm, tok_hbm, slot_hbm, tab_hbm, mc_hbm, ms_hbm, vc_hbm, vs_hbm,
    nt, mom, sec, top,
    cot, tok, slot, scales, codes,
    send, recv, grad_acc, peak, peaks,
    in_sems, send_sem, recv_sems, psend_sem, precv_sem, ready, mine, below, go, mp_in, mp_go, pal,
):
    dp, mp = lax.axis_index("dp"), lax.axis_index("mp")
    side = math.isqrt(n_dp)
    r_dp = dp_rank(dp, n_dp)
    level, place_in = r_dp // side, r_dp % side
    hub = level == 0
    middle = side // 2
    not_hub = level > 0
    n_early = side * CUT // 8 * side
    late = (r_dp >= n_early).astype(jnp.int32)
    known = known_to(level, side)
    later = later_than(level, side)
    width, n_tok = cot.shape
    rows = codes.shape[2]
    ms, vs = scales.at[0], scales.at[1]
    mc, vc, tab = codes.at[0], codes.at[1], codes.at[2]
    n_blk = slot.shape[1]
    n_slot = n_dp * CAP
    full = send.shape[2]
    n_meta = full - width
    strip = 48 if width % 48 == 0 else 16

    barrier = pltpu.get_barrier_semaphore()
    partner = mp + 1 - 2 * lax.rem(mp, 2)
    copies = [
        pltpu.make_async_copy(src, dst, in_sems.at[i])
        for i, src, dst in (
            (0, tok_hbm, tok), (1, slot_hbm, slot), (2, cot_hbm, cot),
            (3, ms_hbm, ms), (3, vs_hbm, vs), (4, mc_hbm, mc), (4, vc_hbm, vc), (4, tab_hbm, tab),
        )
    ]
    for copy in copies:
        copy.start()

    def signal(sem, axis, to):
        pl.semaphore_signal(sem, inc=1, device_id={axis: to}, device_id_type=MESH)

    def over_levels(low, high, fn):
        def body(k, _):
            for i in range(side):
                fn(k * side + i)
            return 0

        lax.fori_loop(low, high, body, 0)

    def over_others(fn):
        for i in range(1, side):
            fn(level * side + lax.rem(place_in + i, side))

    def over_mp(fn):
        for i in range(1, n_mp):
            fn(lax.rem(mp + i, n_mp))

    def greet_level(i, _):
        for j in range(side):
            signal(barrier, "dp", dp_at((side - 1 - i) * side + j, n_dp))
        return 0

    lax.fori_loop(0, side - later, greet_level, 0)

    @pl.when(not_hub)
    def _():
        signal(barrier, "mp", partner)

    @pl.when(hub)
    def _():
        over_others(lambda r: signal(barrier, "dp", dp_at(r, n_dp)))
        over_mp(lambda m: signal(barrier, "mp", m))

    pl.semaphore_wait(barrier, jnp.where(hub, side + n_mp - 2, known * side + 1))
    @pl.when(not_hub)
    def _():
        signal(mine.at[level], "dp", dp_at(place_in, n_dp))

    over_levels(0, known, lambda r: signal(ready.at[level], "dp", dp_at(r, n_dp)))

    earlier = (
        lax.broadcasted_iota(jnp.int32, (n_tok, n_tok), 0) < lax.broadcasted_iota(jnp.int32, (n_tok, n_tok), 1)
    ).astype(jnp.bfloat16)
    copies[0].wait()
    copies[1].wait()
    ids = tok[...]
    low = ids % BLOCK
    blk = ids // BLOCK
    in_block = (lax.broadcasted_iota(jnp.int32, (n_blk, n_tok), 0) == blk).astype(jnp.bfloat16)
    slot_rows = jnp.broadcast_to(slot[...].astype(jnp.float32), (16, n_blk)).astype(jnp.bfloat16)
    held = jnp.dot(slot_rows, in_block, preferred_element_type=jnp.float32)[0:1, :].astype(jnp.int32)
    owner = held // 2
    sub = held % 2
    of_owner = (lax.broadcasted_iota(jnp.int32, (n_dp, n_tok), 0) == owner).astype(jnp.float32)
    before = jnp.dot(of_owner.astype(jnp.bfloat16), earlier, preferred_element_type=jnp.float32)
    rank = jnp.sum(of_owner * before, axis=0, keepdims=True)
    place = dp_rank(owner, n_dp) * CAP + rank.astype(jnp.int32)

    meta_row = lax.broadcasted_iota(jnp.int32, (n_meta, n_tok), 0)
    meta = jnp.where(meta_row == 0, low, jnp.where(meta_row == 1, (sub + 1) * BLOCK, 0))
    meta = meta.astype(jnp.float32).astype(jnp.bfloat16)
    copies[2].wait()
    tokens = jnp.concatenate([cot[...], meta], axis=0)

    def fill(first, n):
        slots = lax.broadcasted_iota(jnp.int32, (n * CAP, n_tok), 0) + first * CAP
        chosen = (slots == place).astype(jnp.bfloat16)
        rows_sent = lax.dot_general(chosen, tokens, (((1,), (1,)), ((), ())), preferred_element_type=jnp.float32)
        send[first : first + n] = rows_sent.reshape(n, CAP, full).astype(jnp.bfloat16)

    fill(0, side)

    def rows_to(r):
        to = dp_at(r, n_dp)
        return pltpu.make_async_remote_copy(
            src_ref=send.at[r], dst_ref=recv.at[r_dp], send_sem=send_sem, recv_sem=recv_sems.at[late],
            device_id={"dp": to}, device_id_type=MESH,
        )

    def send_to(r):
        rows_to(r).start()

    over_levels(0, jnp.minimum(known, 1), send_to)

    @pl.when(known > 1)
    def _():
        signal(pal, "mp", partner)

    fill(side, n_dp - side)
    recv[pl.ds(r_dp, 1)] = send[pl.ds(r_dp, 1)]

    pltpu.make_async_copy(scales, scales, in_sems.at[3]).wait()
    pltpu.make_async_copy(codes, codes, in_sems.at[4]).wait()
    for c in range(0, width, strip):
        at = pl.ds(c, strip)
        mom[at, :] = beta_first * (mc[at, :].astype(jnp.float32) * ms[...])
        sec[at, :] = beta_second * (vc[at, :].astype(jnp.float32) * vs[...])

    last_level = level == side - 1

    @pl.when(last_level)
    def _():
        pl.semaphore_wait(below, 1)

    def known_level(k, _):
        pl.semaphore_wait(pal, 1)
        for i in range(side):
            send_to(k * side + i)

        @pl.when(k + 1 < known)
        def _():
            signal(pal, "mp", partner)

        return 0

    lax.fori_loop(1, known, known_level, 0)

    @pl.when(jnp.logical_and(not_hub, jnp.logical_not(last_level)))
    def _():
        pl.semaphore_wait(below, 1)

    over_levels(known, jnp.where(hub, 0, jnp.minimum(level, middle)), send_to)
    @pl.when(not_hub)
    def _():
        pl.semaphore_wait(go.at[0], 1)

    over_levels(middle, level, send_to)
    over_others(send_to)

    for i in range(1, SPREAD):

        @pl.when(jnp.logical_and(not_hub, level + i < later))
        def _():
            pl.semaphore_wait(go.at[i], 1)
            for j in range(side):
                send_to((level + i) * side + j)

    def tell_below(k):
        pl.semaphore_wait(mine.at[k], 1)
        signal(below, "dp", dp_at(k * side + place_in, n_dp))

    def next_level(k, _):
        @pl.when(jnp.logical_and(hub, k <= middle))
        def _():
            tell_below(k)

        @pl.when(jnp.logical_and(hub, k == middle))
        def _():
            for j in range(middle + 1, side):
                tell_below(j)

        pl.semaphore_wait(ready.at[k], side)
        for i in range(side):
            send_to(k * side + i)

        @pl.when(hub)
        def _():
            for i in range(SPREAD):

                @pl.when(jnp.logical_and(k > i, k < later_than(k - i, side)))
                def _():
                    signal(go.at[i], "dp", dp_at((k - i) * side + place_in, n_dp))

            over_mp(lambda m: signal(mp_in, "mp", m))

        return 0

    lax.fori_loop(later, side, next_level, 0)
    others = pl.ds(0, n_dp - 1)
    last = full - LANES
    pick = (lax.broadcasted_iota(jnp.int32, (LANES, rows), 0) >= width - last).astype(jnp.bfloat16)

    def wait_rows(part, n):
        @pl.when(late == part)
        def _():
            pltpu.make_async_copy(recv.at[pl.ds(0, n - 1)], recv.at[pl.ds(0, n - 1)], recv_sems.at[part]).wait()

        @pl.when(late != part)
        def _():
            pltpu.make_async_copy(recv.at[pl.ds(0, n)], recv.at[pl.ds(0, n)], recv_sems.at[part]).wait()

    def sum_rows(first, n):
        got = recv[first : first + n].astype(jnp.float32).reshape(n * CAP, full).astype(jnp.bfloat16)
        index = jnp.dot(got[:, last:full], pick, preferred_element_type=jnp.float32).astype(jnp.int32)
        row = lax.broadcasted_iota(jnp.int32, (n * CAP, rows), 1) + BLOCK
        selector = (row == index).astype(jnp.bfloat16)
        return lax.dot_general(got, selector, (((0,), (0,)), ((), ())), preferred_element_type=jnp.float32)

    wait_rows(0, n_early)
    grad_acc[...] = sum_rows(0, n_early)
    wait_rows(1, n_dp - n_early)
    grad = sum_rows(n_early, n_dp - n_early)

    m_top = jnp.zeros((8, rows), jnp.float32)
    v_top = jnp.zeros((8, rows), jnp.float32)
    for c in range(0, width, strip):
        at = pl.ds(c, strip)
        g = grad_acc[at, :] + grad[c : c + strip]
        moment = mom[at, :] + 0.1 * g
        second = sec[at, :] + 0.05 * (g * g)
        mom[at, :] = moment
        sec[at, :] = second
        m_top = jnp.maximum(m_top, jnp.max(jnp.abs(moment).reshape(strip // 8, 8, rows), axis=0))
        v_top = jnp.maximum(v_top, jnp.max(second.reshape(strip // 8, 8, rows), axis=0))
    peak[0:1, :] = jnp.max(m_top, axis=0, keepdims=True)
    peak[1:2, :] = jnp.max(v_top, axis=0, keepdims=True)

    @pl.when(not_hub)
    def _():
        pl.semaphore_wait(mp_go, 1)

    def send_peak(to):
        pltpu.make_async_remote_copy(
            src_ref=peak, dst_ref=peaks.at[mp], send_sem=psend_sem, recv_sem=precv_sem,
            device_id={"mp": to}, device_id_type=MESH,
        ).start()

    chips = n_mp // 2
    for i in sorted(range(chips), key=lambda i: -min(i, chips - i)):
        for core in (0, 1):
            if i or core:
                send_peak(lax.rem(mp // 2 + i, chips) * 2 + lax.rem(mp + core, 2))
    peaks[pl.ds(mp, 1)] = peak[...][None]

    for c in range(0, width, strip):
        at = pl.ds(c, strip)
        moment, second = mom[at, :], sec[at, :]
        nt[at, :] = (tab[at, :].astype(jnp.float32) - step_rate * (moment / (jnp.sqrt(second) + eps_root))).astype(jnp.bfloat16)

    @pl.when(hub)
    def _():
        pl.semaphore_wait(mp_in, (n_mp - 1) * (side - 1))
        for k in range(1, side):
            signal(mp_go, "dp", dp_at(k * side + place_in, n_dp))

    pltpu.make_async_copy(send.at[others], send.at[others], send_sem).wait()
    others = pl.ds(0, n_mp - 1)
    pltpu.make_async_copy(peaks.at[others], peaks.at[others], precv_sem).wait()
    top[...] = jnp.max(peaks[...], axis=0)
    pltpu.make_async_copy(peaks.at[others], peaks.at[others], psend_sem).wait()


def strips(width):
    strip = 48 if width % 48 == 0 else 16
    return [pl.ds(c, strip) for c in range(0, width, strip)]


def write(
    nt, mom, sec, top,
    nt_hbm, nm_hbm, nms_hbm, nv_hbm, nvs_hbm,
    nm, nv, nms, nvs, sems,
):
    width = nt.shape[0]
    m_peak, v_peak = top[0:1], top[1:2]
    nms[...] = m_peak
    nvs[...] = v_peak
    parts = strips(width)

    def put(src, dst, sem, at):
        pltpu.make_async_copy(src.at[at], dst.at[at], sems.at[sem]).start()

    for at in parts:
        put(nt, nt_hbm, 0, at)
    lines = [pltpu.make_async_copy(nms, nms_hbm, sems.at[3]), pltpu.make_async_copy(nvs, nvs_hbm, sems.at[4])]
    for line in lines:
        line.start()
    m_peak, v_peak = m_peak + eps_peak, v_peak + eps_peak
    for at in parts:
        nm[at, :] = (mom[at, :] / m_peak).astype(jnp.bfloat16)
        put(nm, nm_hbm, 1, at)
        nv[at, :] = (sec[at, :] / v_peak).astype(jnp.bfloat16)
        put(nv, nv_hbm, 2, at)
    for i, (src, dst) in enumerate(((nt, nt_hbm), (nm, nm_hbm), (nv, nv_hbm))):
        pltpu.make_async_copy(src, dst, sems.at[i]).wait()
    for line in lines:
        line.wait()


def per_device(cotangent, token_ids, block_counts, block_slot, table, m_code, m_scale, v_code, v_scale):
    del block_counts
    n_dp, n_mp = lax.axis_size("dp"), lax.axis_size("mp")
    n_tok, width = cotangent.shape
    rows = table.shape[0]
    full = width // LANES * LANES + LANES
    bf, f32, i32 = jnp.bfloat16, jnp.float32, jnp.int32
    wide, line = (width, rows), (1, rows)
    side = math.isqrt(n_dp)
    hbm = pl.BlockSpec(memory_space=pltpu.HBM)
    vmem = pl.BlockSpec(memory_space=pltpu.VMEM)
    operands = (
        cotangent.T, token_ids.reshape(1, -1), block_slot.reshape(1, -1), table.T,
        m_code.T, m_scale.reshape(line), v_code.T, v_scale.reshape(line),
    )
    operands = [pltpu.with_memory_space_constraint(x, pltpu.HBM) for x in operands]
    held = pl.pallas_call(
        functools.partial(exchange, n_dp, n_mp),
        out_shape=(pltpu.VMEM(wide, bf), pltpu.VMEM(wide, f32), pltpu.VMEM(wide, f32), pltpu.VMEM((2, rows), f32)),
        in_specs=[hbm] * 8,
        out_specs=[vmem] * 4,
        scratch_shapes=[
            pltpu.VMEM((width, n_tok), bf),
            pltpu.VMEM((1, n_tok), i32),
            pltpu.VMEM((1, block_slot.shape[0]), i32),
            pltpu.VMEM((2, 1, rows), f32),
            pltpu.VMEM((3, *wide), bf),
            pltpu.VMEM((n_dp, CAP, full), bf),
            pltpu.VMEM((n_dp, CAP, full), bf),
            pltpu.VMEM((full, rows), f32),
            pltpu.VMEM((2, rows), f32),
            pltpu.VMEM((n_mp, 2, rows), f32),
            pltpu.SemaphoreType.DMA((5,)),
            pltpu.SemaphoreType.DMA,
            pltpu.SemaphoreType.DMA((2,)),
            pltpu.SemaphoreType.DMA,
            pltpu.SemaphoreType.DMA,
            pltpu.SemaphoreType.REGULAR((side,)),
            pltpu.SemaphoreType.REGULAR((side,)),
            pltpu.SemaphoreType.REGULAR,
            pltpu.SemaphoreType.REGULAR((SPREAD,)),
            pltpu.SemaphoreType.REGULAR,
            pltpu.SemaphoreType.REGULAR,
            pltpu.SemaphoreType.REGULAR,
        ],
        compiler_params=pltpu.CompilerParams(
            collective_id=0, has_side_effects=True, vmem_limit_bytes=32 * 1024 * 1024
        ),
        name="embed_adam",
    )(*operands)
    new_table, new_m_code, new_m_scale, new_v_code, new_v_scale = pl.pallas_call(
        write,
        out_shape=(
            jax.ShapeDtypeStruct(wide, bf),
            jax.ShapeDtypeStruct(wide, bf),
            jax.ShapeDtypeStruct(line, f32),
            jax.ShapeDtypeStruct(wide, bf),
            jax.ShapeDtypeStruct(line, f32),
        ),
        in_specs=[vmem] * 4,
        out_specs=[hbm] * 5,
        scratch_shapes=[
            pltpu.VMEM(wide, bf),
            pltpu.VMEM(wide, bf),
            pltpu.VMEM(line, f32),
            pltpu.VMEM(line, f32),
            pltpu.SemaphoreType.DMA((5,)),
        ],
        compiler_params=pltpu.CompilerParams(vmem_limit_bytes=16 * 1024 * 1024),
        name="codes",
    )(*held)
    return (new_table.T, new_m_code.T, new_m_scale.reshape(rows), new_v_code.T, new_v_scale.reshape(rows))


def solution(mesh):
    return jax.shard_map(
        per_device,
        mesh=mesh,
        in_specs=(
            P("dp", "mp"),
            P("dp"),
            P("dp", None),
            P(),
            P("dp", "mp"),
            P("dp", "mp"),
            P("dp"),
            P("dp", "mp"),
            P("dp"),
        ),
        out_specs=(P("dp", "mp"), P("dp", "mp"), P("dp"), P("dp", "mp"), P("dp")),
        check_vma=False,
    )
```
